32 devices in a mesh: expert: 8 (over y, x, core), dp: 4 (over z).
Axes of the slice: x: 2, y: 2, z: 4, core: 2. Of those that a mesh axis runs over, the one named last changes fastest.
Arguments:
- tokens: bfloat16 [1024, 4096], P('expert', 'dp'), may hold values from -6 to 6
- cotangent: bfloat16 [1024, 4096], P('expert', 'dp'), may hold values from -6 to 6
- gate_probs: bfloat16 [1024, 8], P('expert'), may hold values from 0.019897461 to 0.3984375
- expert_ids: int32 [1024, 8], P('expert'), may hold values from 0 to 31, all different within a row; in each aligned block of 128 rows (0 to 127, 128 to 255, ...) at most 36 rows name the same one
- gate_weight: bfloat16 [32, 4096, 1024], P('expert', 'dp'), may hold values from -0.09375 to 0.09375
- up_weight: bfloat16 [32, 4096, 1024], P('expert', 'dp'), may hold values from -0.09375 to 0.09375
- down_weight: bfloat16 [32, 1024, 4096], P('expert', None, 'dp'), may hold values from -0.1875 to 0.1875
Outputs:
- grad_tokens: bfloat16 [1024, 4096], P('expert', 'dp')
- grad_gates: float32 [1024, 8], P('expert')
- grad_gate_weight: float32 [32, 4096, 1024], P('expert', 'dp')
- grad_up_weight: float32 [32, 4096, 1024], P('expert', 'dp')
- grad_down_weight: float32 [32, 1024, 4096], P('expert', None, 'dp')
The draws below stay inside these ranges and needn't reach their ends.
Inputs may be any that keep to these rules, and one draw needn't show every extreme that they name: `expert_ids`: each row names 8 different experts. Among the 128 rows of one group no expert is named more than 36 times, and in every draw some expert is named exactly 36 times by the rows of some group.
All inputs are finite; a program needn't handle non-finite values.
Results may differ from the reference program's by a relative error of at most 0.012.
Values may be sent and summed in bfloat16 or wider, within the bound.
No kernel may reach another device: no remote copies, remote signals or barrier semaphores. Data moves between devices by JAX's collectives and lax.ppermute only.
A program may use at most 192 MiB of HBM per device.

```python
import math
import jax
import jax.numpy as jnp
import numpy as np
from jax import lax

D = 4096
FF = 1024
TOP = 8
EXPERTS = 32
TOK_GRP = 128
CAP = 36
TOKENS = 1024
N_EXPERT = 8
N_DP = 4


def steps_of(rng, dims, shards, least, high):
    def one(axis_at, parts):
        draws = jax.random.uniform(jax.random.fold_in(jax.random.fold_in(rng, 6), axis_at), (parts,), jnp.float32, least / len(shards), high / len(shards))
        return jnp.repeat(jnp.exp(draws), dims[axis_at] // parts).reshape((-1,) + (1,) * (len(dims) - axis_at - 1))

    level = one(*shards[0])
    for cut in shards[1:]:
        level = level * one(*cut)
    return level


def assign_block(own_key, own, number, rows, amount, top, bound, slope):
    sequence = jax.random.permutation(own_key, amount)
    crowded, common = portions_of(amount, rows * top, bound, slope, True), portions_of(amount, rows * top, bound, slope, False)
    places = jnp.arange(amount)

    def named(lengths, offset_by):
        used = int((lengths > 0).sum())
        fixed = max(1, used // 4)
        shifted = fixed + (places - fixed + offset_by * (used - fixed)) % max(1, amount - fixed)
        return jnp.zeros((amount,), jnp.int32).at[sequence[jnp.where(places < fixed, places, shifted)]].set(jnp.asarray(lengths, jnp.int32))

    lengths = jnp.where(number % 4 == 0, named(crowded, number // 4), named(common, number - number // 4 - 1))
    mixed = jax.random.permutation(jax.random.fold_in(own, 3), amount)
    giver, receiver = mixed[0:amount // 2 * 2:2], mixed[1:amount // 2 * 2:2]
    margin = jnp.minimum(lengths[giver] - 1, bound - lengths[receiver]) // 2
    margin = jnp.where((giver == sequence[0]) | (receiver == sequence[0]) | (lengths[receiver] == 0), 0, jnp.maximum(margin, 0))
    shifted = jax.random.randint(jax.random.fold_in(own, 4), (amount // 2,), 0, 1 << 20) % (margin + 1)
    lengths = lengths.at[giver].add(-shifted).at[receiver].add(shifted)
    members = jnp.searchsorted(jnp.cumsum(lengths), jnp.arange(rows * top), side="right").astype(jnp.int32)
    listing = members.reshape(top, rows).T
    listing = listing[jax.random.permutation(jax.random.fold_in(own, 1), rows)]
    offset_by = jax.random.randint(jax.random.fold_in(own, 2), (rows, 1), 0, top)
    return jnp.take_along_axis(listing, (jnp.arange(top)[None, :] + offset_by) % top, axis=1)


def portions_of(amount, total, reach, slope, full):
    loads = [(1 << 20) // math.isqrt(standing ** slope) + 1 for standing in range(1, amount + 1)]
    largest = reach if full else min(reach, max(-(-total // amount), total * loads[0] // sum(loads)))
    least = 1 if total - largest >= amount - 1 else 0
    holding, surplus = [largest] + [least] * (amount - 1), total - largest - least * (amount - 1)
    while surplus > 0:
        movable = [i for i in range(1, amount) if holding[i] < largest] or [i for i in range(1, amount) if holding[i] < reach]
        pool, left = sum([loads[i] for i in movable]), surplus
        for i in movable:
            addition = min(reach - holding[i], max(1, left * loads[i] // pool), surplus)
            holding[i] = holding[i] + addition
            surplus = surplus - addition
    return np.array(holding)


def scatter_about(key, extent, width, bound, split=(), kind=jnp.bfloat16):
    drawn = jax.random.normal(key, extent, jnp.float32) * width
    if len(split) > 0:
        drawn = steps_of(key, extent, split, -0.22, 0.18) * drawn
    return jnp.clip(drawn, min=-bound, max=bound).astype(kind)


def setup_inputs(seed: int = 0) -> dict:
    key_of = jax.random.split(jax.random.key(seed), 8)
    tokens = scatter_about(key_of[0], (TOKENS, D), 1.0, 6.0, ((0, 8), (1, 4)))
    cotangent = scatter_about(key_of[1], (TOKENS, D), 1.0, 6.0, ((0, 8), (1, 4)))
    gate_probs = jnp.clip(jnp.exp(math.log(0.3984375) - 2.9969585 * jax.random.uniform(key_of[2], (TOKENS, TOP), jnp.float32) ** steps_of(key_of[2], (TOKENS, TOP), ((0, 8),), -0.2, 0.2)), 0.019897461, 0.3984375).astype(jnp.bfloat16)
    expert_ids_keys = jax.random.split(jax.random.fold_in(key_of[3], 1), TOKENS // TOK_GRP)
    expert_ids_turns = jax.random.permutation(jax.random.fold_in(key_of[3], 3), TOKENS // TOK_GRP)
    expert_ids = jax.vmap(lambda own, number: assign_block(jax.random.fold_in(key_of[3], 2), own, number, TOK_GRP, EXPERTS, TOP, CAP, 2))(expert_ids_keys, expert_ids_turns).reshape((TOKENS, TOP))
    gate_weight = scatter_about(key_of[4], (EXPERTS, D, FF), D ** -0.5, 0.09375, ((0, 8), (1, 4)))
    up_weight = scatter_about(key_of[5], (EXPERTS, D, FF), D ** -0.5, 0.09375, ((0, 8), (1, 4)))
    down_weight = scatter_about(key_of[6], (EXPERTS, FF, D), FF ** -0.5, 0.1875, ((0, 8), (2, 4)))
    return dict(tokens=tokens, cotangent=cotangent, gate_probs=gate_probs, expert_ids=expert_ids, gate_weight=gate_weight, up_weight=up_weight, down_weight=down_weight)


def expert_reference(operands):
    x_rows, dy_rows, g_rows, gate_w, up_w, down_w = operands
    row_count = x_rows.shape[0]
    gate_pre = jnp.dot(x_rows, gate_w, preferred_element_type=jnp.float32)
    up_pre = jnp.dot(x_rows, up_w, preferred_element_type=jnp.float32)
    back_hidden = jnp.dot(dy_rows, down_w.T, preferred_element_type=jnp.float32)
    sigmoid_gate = jax.nn.sigmoid(gate_pre)
    swish_gate = gate_pre * sigmoid_gate
    hidden = (swish_gate * up_pre).astype(jnp.bfloat16)
    gate_blocks = (back_hidden * hidden.astype(jnp.float32)).reshape(row_count, N_DP, FF // N_DP).sum(-1)
    gate_terms = lax.optimization_barrier(gate_blocks.astype(jnp.bfloat16)).astype(jnp.float32).sum(-1)
    scaled = g_rows.astype(jnp.float32)[:, None]
    grad_hidden = scaled * back_hidden
    derivative = sigmoid_gate * (1.0 + gate_pre * (1.0 - sigmoid_gate))
    grad_gate_pre = (grad_hidden * up_pre * derivative).astype(jnp.bfloat16)
    grad_up_pre = (grad_hidden * swish_gate).astype(jnp.bfloat16)
    input_terms = jnp.dot(grad_gate_pre, gate_w.T, preferred_element_type=jnp.float32)
    input_terms = input_terms + jnp.dot(grad_up_pre, up_w.T, preferred_element_type=jnp.float32)
    input_part = input_terms.astype(jnp.bfloat16)
    scaled_dy = (scaled * dy_rows.astype(jnp.float32)).astype(jnp.bfloat16)
    grad_down = jnp.dot(hidden.T, scaled_dy, preferred_element_type=jnp.float32)
    grad_gate = jnp.dot(x_rows.T, grad_gate_pre, preferred_element_type=jnp.float32)
    grad_up = jnp.dot(x_rows.T, grad_up_pre, preferred_element_type=jnp.float32)
    return input_part, gate_terms, grad_gate, grad_up, grad_down


def reference(tokens, cotangent, gate_probs, expert_ids, gate_weight, up_weight, down_weight):
    group_total = N_EXPERT
    per_group = expert_ids.reshape(group_total, TOK_GRP * TOP)
    columns = jnp.arange(EXPERTS, dtype=jnp.int32)
    member = (per_group[:, :, None] == columns[None, None, :]).astype(jnp.int32)
    ranked = jnp.cumsum(member, axis=1) - 1
    within = jnp.sum(member * ranked, axis=2).astype(jnp.int32)
    group_index = jnp.arange(group_total, dtype=jnp.int32)[:, None]
    position = (group_index * CAP + within).reshape(-1).astype(jnp.int32)
    flat_ids = expert_ids.reshape(-1).astype(jnp.int32)
    row_total = group_total * CAP
    x_repeat = jnp.repeat(tokens, TOP, axis=0)
    dy_repeat = jnp.repeat(cotangent, TOP, axis=0)
    x_buffer = jnp.zeros((EXPERTS, row_total, D), jnp.bfloat16).at[flat_ids, position].set(x_repeat)
    dy_buffer = jnp.zeros((EXPERTS, row_total, D), jnp.bfloat16).at[flat_ids, position].set(dy_repeat)
    g_buffer = jnp.zeros((EXPERTS, row_total), jnp.bfloat16).at[flat_ids, position].set(gate_probs.reshape(-1))
    input_parts, gate_terms, grad_gate, grad_up, grad_down = lax.map(
        expert_reference, (x_buffer, dy_buffer, g_buffer, gate_weight, up_weight, down_weight))
    picked = lax.optimization_barrier(input_parts[flat_ids, position]).astype(jnp.float32)
    grad_tokens = picked.reshape(TOKENS, TOP, D).sum(1).astype(jnp.bfloat16)
    grad_gates = gate_terms[flat_ids, position].reshape(TOKENS, TOP)
    return grad_tokens, grad_gates, grad_gate, grad_up, grad_down
```

```python
import functools

import jax
import jax.numpy as jnp
from jax import lax
from jax.experimental import pallas as pl
from jax.experimental.pallas import tpu as pltpu
from jax.sharding import PartitionSpec as P

TOP = 8
EXPERTS = 32
CAP = 36
VMEM_BYTES = 56 * 1024 * 1024
F32 = jnp.float32
BF16 = jnp.bfloat16
ANY = pl.BlockSpec(memory_space=pl.ANY)


def params():
    return pltpu.CompilerParams(vmem_limit_bytes=VMEM_BYTES)


def nt_dot(a, b):
    return lax.dot_general(a, b, (((1,), (1,)), ((), ())), preferred_element_type=F32)


def forward_body(blocks, me_ref, x_ref, dy_ref, gate_ref, up_ref, down_ref, *rest):
    out_ref, first_ref = rest[-2:]
    step = pl.program_id(1)
    out_ref[0, 0] = jnp.dot(x_ref[...], gate_ref[0], preferred_element_type=F32).astype(BF16)
    out_ref[0, 1] = jnp.dot(x_ref[...], up_ref[0], preferred_element_type=F32).astype(BF16)
    out_ref[0, 2] = nt_dot(dy_ref[...], down_ref[0]).astype(BF16)
    wanted = jnp.where(me_ref[0] == 0, blocks - 1, 1)

    @pl.when(step == wanted)
    def _():
        first_ref[...] = out_ref[0]


def forward(me, x, dy, gate_w, up_w, down_w, start, count, blocks, deps):
    rows = x.shape[0] // count
    width = x.shape[1]
    fb = gate_w.shape[2] // blocks
    total = x.shape[0]
    flops = 6 * total * width * fb * blocks
    return pl.pallas_call(
        functools.partial(forward_body, blocks),
        out_shape=(
            jax.ShapeDtypeStruct((blocks, 3, total, fb), BF16),
            jax.ShapeDtypeStruct((3, total, fb), BF16),
        ),
        grid_spec=pltpu.PrefetchScalarGridSpec(
            num_scalar_prefetch=1,
            grid=(count, blocks),
            in_specs=[
                pl.BlockSpec((rows, width), lambda i, k, m: (i, 0)),
                pl.BlockSpec((rows, width), lambda i, k, m: (i, 0)),
                pl.BlockSpec((1, width, fb), lambda i, k, m: (start + i, 0, (m[0] + k) % blocks)),
                pl.BlockSpec((1, width, fb), lambda i, k, m: (start + i, 0, (m[0] + k) % blocks)),
                pl.BlockSpec((1, fb, width), lambda i, k, m: (start + i, (m[0] + k) % blocks, 0)),
            ]
            + [ANY] * len(deps),
            out_specs=[
                pl.BlockSpec((1, 3, rows, fb), lambda i, k, m: (k, 0, i, 0)),
                pl.BlockSpec((3, rows, fb), lambda i, k, m: (0, i, 0)),
            ],
        ),
        compiler_params=params(),
        cost_estimate=pl.CostEstimate(
            flops=flops, bytes_accessed=count * 6 * width * fb * blocks, transcendentals=0
        ),
        name="forward_products",
    )(me, x, dy, gate_w, up_w, down_w, *deps)


def add_body(pairs, *refs):
    outs = refs[-pairs:]
    for at in range(pairs):
        own, got = refs[2 * at], refs[2 * at + 1]
        outs[at][...] = (own[0].astype(F32) + got[...].astype(F32)).astype(BF16)


def add_blocks(parts, places, received, deps):
    _, three, rows, fb = parts.shape
    pairs = len(places)
    operands, specs = [], []
    for place, got in zip(places, received):
        operands += [parts, got]
        specs += [
            pl.BlockSpec((1, 1, rows, fb), lambda i, place=place: (place, i, 0, 0)),
            pl.BlockSpec((1, rows, fb), lambda i: (i, 0, 0)),
        ]
    return pl.pallas_call(
        functools.partial(add_body, pairs),
        out_shape=[jax.ShapeDtypeStruct((three, rows, fb), BF16)] * pairs,
        grid=(three,),
        in_specs=specs + [ANY] * len(deps),
        out_specs=[pl.BlockSpec((1, rows, fb), lambda i: (i, 0, 0))] * pairs,
        compiler_params=params(),
        cost_estimate=pl.CostEstimate(
            flops=pairs * three * rows * fb,
            bytes_accessed=pairs * 6 * three * rows * fb,
            transcendentals=0,
        ),
        name="hop_sum",
    )(*operands, *deps)


def join_body(a_ref, b_ref, *rest):
    rest[-1][...] = a_ref[...] + b_ref[...]


def join(a, b, deps):
    return pl.pallas_call(
        join_body,
        out_shape=jax.ShapeDtypeStruct(a.shape, BF16),
        in_specs=[pl.BlockSpec(memory_space=pltpu.VMEM)] * 2 + [ANY] * len(deps),
        out_specs=pl.BlockSpec(memory_space=pltpu.VMEM),
        compiler_params=params(),
        cost_estimate=pl.CostEstimate(
            flops=a.size, bytes_accessed=6 * a.size, transcendentals=0
        ),
        name="hop_join",
    )(a, b, *deps)


def hidden_body(own_ref, right_ref, left_ref, g_ref, *rest):
    out_ref = rest[-1]
    rows = right_ref.shape[1]

    def total(at):
        return (
            own_ref[0, at].astype(F32) + right_ref[at].astype(F32) + left_ref[at].astype(F32)
        )

    gate, up, back = total(0), total(1), total(2)
    sig = jax.nn.sigmoid(gate)
    swish = gate * sig
    hidden = (swish * up).astype(BF16)
    product = back * hidden.astype(F32)
    grad = g_ref[...] * back
    out_ref[0:rows] = hidden
    out_ref[rows : 2 * rows] = (grad * up * (sig * (1.0 + gate * (1.0 - sig)))).astype(BF16)
    out_ref[2 * rows : 3 * rows] = (grad * swish).astype(BF16)
    high = product.astype(BF16)
    low = (product - high.astype(F32)).astype(BF16)
    fb = product.shape[1]
    ones = jnp.ones((16, fb), BF16)
    for part in range(-(-rows // fb)):
        lo, hi = part * fb, min(rows, part * fb + fb)
        sums = nt_dot(ones, high[lo:hi]) + nt_dot(ones, low[lo:hi])
        base = 3 * rows + 16 * part
        if hi - lo < fb:
            out_ref[base : base + 16] = jnp.zeros((16, fb), BF16)
        out_ref[base : base + 16, 0 : hi - lo] = sums.astype(BF16)


def hidden_units(parts, right, left, g_rows, deps):
    three, rows, fb = right.shape
    return pl.pallas_call(
        hidden_body,
        out_shape=jax.ShapeDtypeStruct((3 * rows + 16 * (-(-rows // fb)), fb), BF16),
        grid=(1,),
        in_specs=[
            pl.BlockSpec((1, 3, rows, fb), lambda i: (0, 0, 0, 0)),
            pl.BlockSpec((3, rows, fb), lambda i: (0, 0, 0)),
            pl.BlockSpec((3, rows, fb), lambda i: (0, 0, 0)),
            pl.BlockSpec((rows, 1), lambda i: (0, 0)),
        ]
        + [ANY] * len(deps),
        out_specs=pl.BlockSpec((3 * rows + 16 * (-(-rows // fb)), fb), lambda i: (0, 0)),
        compiler_params=params(),
        cost_estimate=pl.CostEstimate(
            flops=30 * rows * fb, bytes_accessed=24 * rows * fb, transcendentals=rows * fb
        ),
        name="hidden_units",
    )(parts, right, left, g_rows, *deps)


def pass_body(*refs):
    pass


def pass_on(a, b, deps):
    shape = jax.ShapeDtypeStruct(a.shape, a.dtype)
    return pl.pallas_call(
        pass_body,
        out_shape=[shape, shape],
        in_specs=[ANY] * (2 + len(deps)),
        out_specs=[ANY, ANY],
        input_output_aliases={0: 0, 1: 1},
        compiler_params=params(),
        cost_estimate=pl.CostEstimate(flops=0, bytes_accessed=0, transcendentals=0),
        name="hop_forward",
    )(a, b, *deps)


def expert_body(place, near_rows, far_rows, aliased, me_ref, *refs):
    near, far = refs[0:5], refs[5:10]
    near_x, near_dy, far_x, far_dy, gate_ref, up_ref = refs[10:16]
    grad_gate, grad_up, grad_down, rows_ref = refs[-8:-4]
    act, xs, dys, total = refs[-4:]
    step = pl.program_id(0)
    last = pl.num_programs(0) - 1
    me = me_ref[0]
    near_total = near_x.shape[0]
    at = place * near_rows

    def fill(which):
        for j in range(3):
            act[j, 0:near_rows] = near[which][pl.ds(j * near_total + at, near_rows)]
            act[j, near_rows:] = far[which][pl.ds(j * far_rows, far_rows)]

    @pl.when(step == 0)
    def _():
        fill(0)
        xs[0:near_rows] = near_x[pl.ds(at, near_rows)]
        xs[near_rows:] = far_x[...]
        dys[0:near_rows] = near_dy[pl.ds(at, near_rows)]
        dys[near_rows:] = far_dy[...]
        total[...] = jnp.zeros_like(total)

    @pl.when((step == 1) & (me != last))
    def _():
        fill(1)

    @pl.when((step == last) & (me != 0))
    def _():
        fill(2)

    @pl.when(step == 2)
    def _():
        fill(3)

    @pl.when(((step == 1) & (me == last)) | ((step == last) & (me == 0)))
    def _():
        fill(4)

    hidden, gate_grad, up_grad = act[0], act[1], act[2]
    total[...] += nt_dot(gate_grad, gate_ref[0]) + nt_dot(up_grad, up_ref[0])

    @pl.when(step == last)
    def _():
        rows_ref[...] = total[...].astype(BF16)

    over_rows = (((0,), (0,)), ((), ()))
    grad_gate[0] = lax.dot_general(xs[...], gate_grad, over_rows, preferred_element_type=F32)
    grad_up[0] = lax.dot_general(xs[...], up_grad, over_rows, preferred_element_type=F32)
    grad_down[0] = lax.dot_general(hidden, dys[...], over_rows, preferred_element_type=F32)


def expert_grads(me, place, near, far, near_x, near_dy, far_x, far_dy, weights, earlier, deps):
    gate_w, up_w = weights
    experts, width, ff = gate_w.shape
    fb = near[0].shape[1]
    blocks = ff // fb
    near_rows = near_x.shape[0] // experts
    far_rows = far_x.shape[0]
    rows = near_rows + far_rows

    def whole(a):
        return pl.BlockSpec(a.shape, lambda k, m: (0,) * a.ndim, pipeline_mode=pl.Buffered(1))

    wide = pl.BlockSpec((1, width, fb), lambda k, m: (place, 0, (m[0] + k) % blocks))
    tall = pl.BlockSpec((1, fb, width), lambda k, m: (place, (m[0] + k) % blocks, 0))
    held = [*near, *far, near_x, near_dy, far_x, far_dy]
    operands = [me, *held, gate_w, up_w]
    specs = [whole(a) for a in held] + [wide, wide]
    aliases = {}
    if earlier is not None:
        aliases = {len(operands) + j: j for j in range(3)}
        operands += list(earlier)
        specs += [ANY] * 3
    return pl.pallas_call(
        functools.partial(expert_body, place, near_rows, far_rows, earlier is not None),
        out_shape=(
            jax.ShapeDtypeStruct((experts, width, ff), F32),
            jax.ShapeDtypeStruct((experts, width, ff), F32),
            jax.ShapeDtypeStruct((experts, ff, width), F32),
            jax.ShapeDtypeStruct((rows, width), BF16),
        ),
        grid_spec=pltpu.PrefetchScalarGridSpec(
            num_scalar_prefetch=1,
            grid=(blocks,),
            in_specs=specs + [ANY] * len(deps),
            out_specs=[wide, wide, tall, pl.BlockSpec((rows, width), lambda k, m: (0, 0))],
            scratch_shapes=[
                pltpu.VMEM((3, rows, fb), BF16),
                pltpu.VMEM((rows, width), BF16),
                pltpu.VMEM((rows, width), BF16),
                pltpu.VMEM((rows, width), F32),
            ],
        ),
        input_output_aliases=aliases,
        compiler_params=params(),
        cost_estimate=pl.CostEstimate(
            flops=10 * rows * width * ff, bytes_accessed=16 * width * ff, transcendentals=0
        ),
        name="expert_grads",
    )(*operands, *deps)


def swap(array, bit, count):
    return lax.ppermute(array, "expert", [(i, i ^ (1 << bit)) for i in range(count)])


def spread(own, order, count):
    held = own[None]
    for bit in order:
        held = jnp.concatenate([held, swap(held, bit, count)])
    return held


def offsets(order):
    held = [0]
    for bit in order:
        held = held + [at | (1 << bit) for at in held]
    return held


def reordered(array, have, want):
    if have == want:
        return array
    return jnp.stack([array[have.index(at)] for at in want])


def shards(tokens, cotangent, gate_probs, expert_ids, gate_weight, up_weight, down_weight):
    count = lax.axis_size("expert")
    blocks = lax.axis_size("dp")
    me = lax.axis_index("dp").astype(jnp.int32)
    group = lax.axis_index("expert").astype(jnp.int32)
    me_arg = me.reshape(1)
    local = gate_weight.shape[0]
    group_size, width = tokens.shape
    fb = gate_weight.shape[2] // blocks
    bits = count.bit_length() - 1
    pair = 2

    meta_rows = -(-group_size * TOP // width)
    pad_rows = -(-2 * meta_rows // 16) * 16

    def as_rows(a):
        flat = jnp.pad(a.astype(BF16).reshape(-1), (0, meta_rows * width - a.size))
        return flat.reshape(meta_rows, width)

    meta = jnp.concatenate(
        [
            as_rows(expert_ids),
            as_rows(gate_probs),
            jnp.zeros((pad_rows - 2 * meta_rows, width), BF16),
        ]
    )
    own_x = jnp.concatenate([tokens, meta])
    near_x_all = jnp.stack([own_x, swap(own_x, 0, count)])
    near_dy_all = jnp.stack([cotangent, swap(cotangent, 0, count)])
    ahead = list(range(1, bits))
    chips_x = spread(own_x, ahead, count)
    chips_dy = spread(cotangent, ahead[::-1], count)
    even = [at for at in range(0, count, 2)]
    chips_dy = reordered(chips_dy, offsets(ahead[::-1]), even)
    far_x_all = jnp.stack([chips_x[1:], swap(chips_x[1:], 0, count)], axis=1)
    far_dy_all = jnp.stack([chips_dy[1:], swap(chips_dy[1:], 0, count)], axis=1)
    far_x_all = far_x_all.reshape((count - pair,) + own_x.shape)
    far_dy_all = far_dy_all.reshape((count - pair,) + cotangent.shape)

    def meta_of(a, which):
        part = a[:, group_size + which * meta_rows : group_size + (which + 1) * meta_rows]
        part = part.reshape(a.shape[0], -1)[:, : group_size * TOP]
        return part.reshape(a.shape[0], group_size, TOP)

    experts_here = (group * local + jnp.arange(local, dtype=jnp.int32)).astype(F32)
    before = (
        jnp.arange(group_size)[:, None] < jnp.arange(group_size)[None, :]
    ).astype(BF16)

    def members(a):
        named = meta_of(a, 0).astype(F32)[None] == experts_here[:, None, None, None]
        member = jnp.any(named, axis=3)
        prob = jnp.sum(jnp.where(named, meta_of(a, 1).astype(F32)[None], 0.0), axis=3)
        ranks = jnp.einsum(
            "egt,tu->egu", member.astype(BF16), before, preferred_element_type=F32
        ).astype(jnp.int32)
        return member, prob, ranks

    near_rows = pair * CAP // 16 * 16
    spill = pair * CAP - near_rows
    far_rows = -(-(spill + (count - pair) * CAP) // 16) * 16

    near_member, near_prob, near_rank = members(near_x_all)
    held = jnp.sum(near_member[:, :1].astype(jnp.int32), axis=2, keepdims=True)
    near_rank = jnp.concatenate([near_rank[:, :1], near_rank[:, 1:] + held], axis=1)
    near_rank = jnp.where(near_member, near_rank, -1).reshape(local, -1)
    near_prob = near_prob.reshape(local, -1)
    near_tokens = near_x_all[:, :group_size].reshape(-1, width)
    near_cot = near_dy_all.reshape(-1, width)

    def pick(slot, rows):
        return slot[None, :] == jnp.arange(rows, dtype=jnp.int32)[:, None]

    def gather(chosen, prob, x_all, dy_all):
        hot = chosen.astype(BF16)
        x = jnp.dot(hot, x_all, preferred_element_type=F32).astype(BF16)
        dy32 = jnp.dot(hot, dy_all, preferred_element_type=F32)
        g = jnp.sum(jnp.where(chosen, prob, 0.0), axis=1, keepdims=True)
        return x, dy32.astype(BF16), (dy32 * g).astype(BF16), g

    near_chosen = jnp.concatenate([pick(near_rank[e], near_rows) for e in range(local)])
    near_prob_rows = jnp.repeat(near_prob, near_rows, axis=0)
    near = gather(near_chosen, near_prob_rows, near_tokens, near_cot)

    far_member, far_prob, far_rank = members(far_x_all)
    first = spill + CAP * jnp.arange(count - pair, dtype=jnp.int32)[None, :, None]
    far_slot = jnp.where(far_member, far_rank + first, -1).reshape(local, -1)
    all_slot = jnp.concatenate([jnp.maximum(near_rank - near_rows, -1), far_slot], axis=1)
    all_prob = jnp.concatenate([near_prob, far_prob.reshape(local, -1)], axis=1)
    all_tokens = jnp.concatenate([near_tokens, far_x_all[:, :group_size].reshape(-1, width)])
    all_cot = jnp.concatenate([near_cot, far_dy_all.reshape(-1, width)])

    chunks = [near]
    for e in range(local):
        chosen = pick(all_slot[e], far_rows)
        chunks.append(gather(chosen, all_prob[e][None, :], all_tokens, all_cot))

    up1 = [(0, 1), (blocks - 1, blocks - 2)]
    up2, down2 = [(0, 1), (1, 2)], [(3, 2), (2, 1)]
    up, down = [(0, 1), (1, 2), (2, 3)], [(1, 0), (2, 1), (3, 2)]
    on, back = [(1, 2), (2, 3)], [(2, 1), (1, 0)]
    ends = [(2, 3), (1, 0)]

    def move(a, pairs):
        return lax.ppermute(a, "dp", pairs)

    total_chunks = local + 1
    state = [dict() for _ in range(total_chunks)]
    chain = []
    grads = None
    row_terms = []

    for window in range(2 * (total_chunks - 1) + 7):
        events = [(c, window - 2 * c) for c in range(total_chunks)]
        events = [ev for ev in events if 0 <= ev[1] <= 6]
        events.sort(key=lambda ev: (ev[1] == 6, ev[0]))
        for c, hop in events:
            s = state[c]
            if hop == 0:
                x, dy, _, _ = chunks[c]
                start, amount = (0, local) if c == 0 else (c - 1, 1)
                s["parts"], first_send = forward(
                    me_arg, x, dy, gate_weight, up_weight, down_weight, start, amount, blocks,
                    chain,
                )
                chain = [first_send]
                s["in"] = move(first_send, up1)
            elif hop == 1:
                (send,) = add_blocks(s["parts"], (2,), (s["in"],), chain)
                chain = [send]
                s["right"], s["left"] = move(send, up2), move(send, down2)
            elif hop == 2:
                right, left = add_blocks(
                    s["parts"], (1, 3), (s["right"], s["left"]), chain
                )
                chain = [right]
                s["right"], s["left"] = move(right, up), move(left, down)
            elif hop == 3:
                s["own"] = hidden_units(
                    s["parts"], s["right"], s["left"], chunks[c][3], chain
                )
                chain = [s["own"]]
                s["r1"], s["l1"] = move(s["own"], up), move(s["own"], down)
            elif hop == 4:
                s["r1"], s["l1"] = pass_on(s["r1"], s["l1"], chain)
                chain = [s["r1"]]
                s["r2"], s["l2"] = move(s["r1"], on), move(s["l1"], back)
            elif hop == 5:
                s["g2"] = join(s["r2"], s["l2"], chain)
                chain = [s["g2"]]
                s["x3"] = move(s["g2"], ends)
            else:
                s["all"] = [s[name] for name in ("own", "l1", "r1", "g2", "x3")]
                if c == 0:
                    continue
                *grads, rows = expert_grads(
                    me_arg, c - 1, state[0]["all"], s["all"], near[0], near[2],
                    chunks[c][0], chunks[c][2], (gate_weight, up_weight), grads, chain,
                )
                chain = [rows]
                row_terms.append(rows)

    def gate_sums(c):
        rows = chunks[c][0].shape[0]
        own, l1, r1, g2, x3 = [
            a[3 * rows :].reshape(-1, 16, fb)[:, 0].reshape(-1)[:rows].astype(F32)
            for a in state[c]["all"]
        ]
        one = jnp.where(me == blocks - 1, x3, l1)
        three = jnp.where(me == 0, x3, r1)
        return own + g2 + one + three

    near_gates = gate_sums(0).reshape(local, near_rows)

    near_size = pair * group_size
    token_terms = 0.0
    gate_terms = []
    for e in range(local):
        near_slot = jnp.where(near_rank[e] >= near_rows, -1, near_rank[e])
        near_slot = jnp.concatenate(
            [near_slot, jnp.full(((count - pair) * group_size,), -1, jnp.int32)]
        )
        slot = jnp.where(
            near_slot >= 0, near_slot, jnp.where(all_slot[e] >= 0, all_slot[e] + near_rows, -1)
        )
        chosen = pick(slot, near_rows + far_rows)
        token_terms = token_terms + lax.dot_general(
            chosen.astype(BF16), row_terms[e], (((0,), (0,)), ((), ())),
            preferred_element_type=F32,
        )
        gates = jnp.concatenate([near_gates[e], gate_sums(e + 1)])
        gate_terms.append(jnp.sum(jnp.where(chosen, gates[:, None], 0.0), axis=0))

    gate_table = jnp.stack(gate_terms, axis=1).reshape(count, group_size, local)
    gate_table = gate_table.transpose(0, 2, 1).reshape(count, local * group_size)
    table_rows = -(-EXPERTS * group_size // width)
    table_pad = -(-table_rows // 16) * 16
    placed = lax.dynamic_update_slice(
        jnp.zeros((count, table_pad * width), BF16),
        gate_table.astype(BF16),
        (jnp.int32(0), group * local * group_size),
    ).reshape(count, table_pad, width)
    terms = token_terms.astype(BF16).reshape(count, group_size, width)
    terms = jnp.concatenate([terms, placed], axis=1)

    def plus(a, b):
        return (a.astype(F32) + b.astype(F32)).astype(BF16)

    by_chip = terms.reshape(count // 2, 2, group_size + table_pad, width)
    held = plus(by_chip[:, 0], swap(by_chip[:, 1], 0, count))

    def settle(part, order):
        have = even
        for at, bit in enumerate(order):
            keep = [i for i, o in enumerate(have) if not o >> bit & 1]
            send = [i for i, o in enumerate(have) if o >> bit & 1]
            partner = [have.index(have[i] | (1 << bit)) for i in keep]
            got = swap(jnp.stack([part[i] for i in partner]), bit, count)
            kept = jnp.stack([part[i] for i in keep])
            last = at == len(order) - 1
            part = kept.astype(F32) + got.astype(F32)
            part = part if last else part.astype(BF16)
            have = [have[i] for i in keep]
        return part[0]

    half = width // 2
    settled = jnp.concatenate(
        [settle(held[..., :half], ahead), settle(held[..., half:], ahead[::-1])], axis=1
    )
    grad_tokens = settled[:group_size].astype(BF16)
    table = settled[group_size:].reshape(-1)[: EXPERTS * group_size]
    table = table.reshape(EXPERTS, group_size).T
    named = expert_ids[:, :, None] == jnp.arange(EXPERTS, dtype=jnp.int32)
    grad_gates = jnp.sum(jnp.where(named, table[:, None, :], 0.0), axis=2)
    return (grad_tokens, grad_gates, *grads)


def solution(mesh):
    placed = (
        P("expert", "dp"),
        P("expert", "dp"),
        P("expert", None),
        P("expert", None),
        P("expert", "dp", None),
        P("expert", "dp", None),
        P("expert", None, "dp"),
    )
    return jax.shard_map(
        shards,
        mesh=mesh,
        in_specs=placed,
        out_specs=(
            P("expert", "dp"),
            P("expert", None),
            P("expert", "dp", None),
            P("expert", "dp", None),
            P("expert", None, "dp"),
        ),
        check_vma=False,
    )
```

```python
import functools

import jax
import jax.numpy as jnp
from jax import lax
from jax.experimental import pallas as pl
from jax.experimental.pallas import tpu as pltpu
from jax.sharding import PartitionSpec as P

TOP = 8
EXPERTS = 32
CAP = 36
MIB = 1024 * 1024
FORWARD_VMEM = 40 * MIB
PAIR = 3.6
WITHIN = 0.5
F32 = jnp.float32
BF16 = jnp.bfloat16
ANY = pl.BlockSpec(memory_space=pl.ANY)
VMEM = pl.BlockSpec(memory_space=pltpu.VMEM)


def params(need):
    return pltpu.CompilerParams(vmem_limit_bytes=min(60 * MIB, need + need // 4 + 4 * MIB))


def nt_dot(a, b):
    return lax.dot_general(a, b, (((1,), (1,)), ((), ())), preferred_element_type=F32)


def forward_body(me_ref, x_ref, dy_ref, gate_ref, up_ref, down_ref, *rest):
    outs = rest[-4:]
    fb = outs[0].shape[2]
    x, dy = x_ref[...], dy_ref[...]
    for at in range(4):
        block = pl.ds(pl.multiple_of((me_ref[0] ^ at) * fb, fb), fb)
        gate = jnp.dot(x, gate_ref[0, :, block], preferred_element_type=F32)
        up = jnp.dot(x, up_ref[0, :, block], preferred_element_type=F32)
        outs[at][0] = gate.astype(BF16)
        outs[at][1] = up.astype(BF16)
        outs[at][2] = nt_dot(dy, down_ref[0, block, :]).astype(BF16)


def forward(me, x, dy, gate_w, up_w, down_w, start, amount, deps):
    total, width = x.shape
    rows = total // amount
    blocks = 4
    ff = gate_w.shape[2]
    fb = ff // blocks
    held = pl.BlockSpec((rows, width), lambda i, m: (i, 0))
    wide = pl.BlockSpec((1, width, ff), lambda i, m: (start + i, 0, 0))
    tall = pl.BlockSpec((1, ff, width), lambda i, m: (start + i, 0, 0))
    part = jax.ShapeDtypeStruct((3, total, fb), BF16)
    return pl.pallas_call(
        forward_body,
        out_shape=[part] * blocks,
        grid_spec=pltpu.PrefetchScalarGridSpec(
            num_scalar_prefetch=1,
            grid=(amount,),
            in_specs=[held, held, wide, wide, tall] + [ANY] * len(deps),
            out_specs=[pl.BlockSpec((3, rows, fb), lambda i, m: (0, i, 0))] * blocks,
        ),
        compiler_params=params(FORWARD_VMEM),
        cost_estimate=pl.CostEstimate(
            flops=6 * total * width * ff,
            bytes_accessed=amount * 6 * width * ff,
            transcendentals=0,
        ),
        name="forward_products",
    )(me, x, dy, gate_w, up_w, down_w, *deps)


def add_body(pairs, *refs):
    outs = refs[-pairs:]
    for at in range(pairs):
        own, got = refs[2 * at], refs[2 * at + 1]
        outs[at][...] = (own[...].astype(F32) + got[...].astype(F32)).astype(BF16)


def add_blocks(terms, deps):
    pairs = len(terms) // 2
    size = terms[0].size
    return pl.pallas_call(
        functools.partial(add_body, pairs),
        out_shape=[jax.ShapeDtypeStruct(terms[0].shape, BF16)] * pairs,
        in_specs=[VMEM] * len(terms) + [ANY] * len(deps),
        out_specs=[VMEM] * pairs,
        compiler_params=params(pairs * 6 * size),
        cost_estimate=pl.CostEstimate(
            flops=pairs * size, bytes_accessed=pairs * 6 * size, transcendentals=0
        ),
        name="hop_sum",
    )(*terms, *deps)


def hidden_body(own_ref, near_ref, far_ref, g_ref, *rest):
    out_ref = rest[-1]
    rows, fb = own_ref.shape[1:]

    def total(at):
        return own_ref[at].astype(F32) + near_ref[at].astype(F32) + far_ref[at].astype(F32)

    gate, up, back = total(0), total(1), total(2)
    sig = jax.nn.sigmoid(gate)
    swish = gate * sig
    hidden = (swish * up).astype(BF16)
    product = back * hidden.astype(F32)
    grad = g_ref[...] * back
    out_ref[0:rows] = hidden
    out_ref[rows : 2 * rows] = (grad * up * (sig * (1.0 + gate * (1.0 - sig)))).astype(BF16)
    out_ref[2 * rows : 3 * rows] = (grad * swish).astype(BF16)
    high = product.astype(BF16)
    low = (product - high.astype(F32)).astype(BF16)
    ones = jnp.ones((16, fb), BF16)
    for part in range(-(-rows // fb)):
        lo, hi = part * fb, min(rows, part * fb + fb)
        sums = nt_dot(ones, high[lo:hi]) + nt_dot(ones, low[lo:hi])
        base = 3 * rows + 16 * part
        if hi - lo < fb:
            out_ref[base : base + 16] = jnp.zeros((16, fb), BF16)
        out_ref[base : base + 16, 0 : hi - lo] = sums.astype(BF16)


def hidden_units(own, near, far, g_rows, deps):
    _, rows, fb = own.shape
    tall = 3 * rows + 16 * (-(-rows // fb))
    return pl.pallas_call(
        hidden_body,
        out_shape=jax.ShapeDtypeStruct((tall, fb), BF16),
        in_specs=[VMEM] * 4 + [ANY] * len(deps),
        out_specs=VMEM,
        compiler_params=params(24 * rows * fb + 48 * rows * fb),
        cost_estimate=pl.CostEstimate(
            flops=30 * rows * fb, bytes_accessed=24 * rows * fb, transcendentals=rows * fb
        ),
        name="hidden_units",
    )(own, near, far, g_rows, *deps)


def pass_body(*refs):
    pass


def pass_on(arrays, deps):
    count = len(arrays)
    return pl.pallas_call(
        pass_body,
        out_shape=[jax.ShapeDtypeStruct(a.shape, a.dtype) for a in arrays],
        in_specs=[ANY] * (count + len(deps)),
        out_specs=[ANY] * count,
        input_output_aliases={at: at for at in range(count)},
        compiler_params=params(0),
        cost_estimate=pl.CostEstimate(flops=0, bytes_accessed=0, transcendentals=0),
        name="hop_forward",
    )(*arrays, *deps)


def take_blocks(step, me, parts, act, kinds):
    middle = (me == 1) | (me == 2)
    rows = act.shape[1]

    def fill_when(wanted, source):
        @pl.when(wanted)
        def _():
            for at, j in enumerate(kinds):
                act[at] = source[pl.ds(j * rows, rows)]

    fill_when(step == 0, parts[0])
    fill_when(step == 1, parts[1])
    fill_when((step == 2) & middle, parts[2])
    fill_when((step == 2) & jnp.logical_not(middle), parts[3])
    fill_when((step == 3) & middle, parts[4])
    fill_when((step == 3) & jnp.logical_not(middle), parts[5])


def rows_body(me_ref, *refs):
    gate_ref, up_ref = refs[6:8]
    rows_ref, act, total = refs[-3:]
    step = pl.program_id(0)
    take_blocks(step, me_ref[0], refs[:6], act, (1, 2))
    terms = nt_dot(act[0], gate_ref[0]) + nt_dot(act[1], up_ref[0])

    @pl.when(step == 0)
    def _():
        total[...] = terms

    @pl.when((step > 0) & (step < 3))
    def _():
        total[...] += terms

    @pl.when(step == 3)
    def _():
        rows_ref[...] = (total[...] + terms).astype(BF16)


def whole(a):
    return pl.BlockSpec(a.shape, lambda k, m: (0,) * a.ndim, pipeline_mode=pl.Buffered(1))


def row_terms_of(me, place, parts, rows, gate_w, up_w, deps):
    _, width, ff = gate_w.shape
    fb = parts[0].shape[1]
    wide = pl.BlockSpec((1, width, fb), lambda k, m: (place, 0, m[0] ^ k))
    need = 2 * sum(a.size for a in parts) + 8 * width * fb + 4 * rows * width
    need += 4 * rows * fb + 16 * rows * width
    return pl.pallas_call(
        rows_body,
        out_shape=jax.ShapeDtypeStruct((rows, width), BF16),
        grid_spec=pltpu.PrefetchScalarGridSpec(
            num_scalar_prefetch=1,
            grid=(ff // fb,),
            in_specs=[whole(a) for a in parts] + [wide, wide] + [ANY] * len(deps),
            out_specs=pl.BlockSpec((rows, width), lambda k, m: (0, 0)),
            scratch_shapes=[
                pltpu.VMEM((2, rows, fb), BF16),
                pltpu.VMEM((rows, width), F32),
            ],
        ),
        compiler_params=params(need),
        cost_estimate=pl.CostEstimate(
            flops=4 * rows * width * ff, bytes_accessed=4 * width * ff, transcendentals=0
        ),
        name="input_terms",
    )(me, *parts, gate_w, up_w, *deps)


def grads_body(me_ref, *refs):
    x_ref, dy_ref = refs[6:8]
    grad_gate, grad_up, grad_down, token, act = refs[-5:]
    step = pl.program_id(0)

    @pl.when(step == 0)
    def _():
        token[...] = jnp.zeros_like(token)

    take_blocks(step, me_ref[0], refs[:6], act, (0, 1, 2))
    over_rows = (((0,), (0,)), ((), ()))
    grad_gate[0] = lax.dot_general(x_ref[...], act[1], over_rows, preferred_element_type=F32)
    grad_up[0] = lax.dot_general(x_ref[...], act[2], over_rows, preferred_element_type=F32)
    grad_down[0] = lax.dot_general(act[0], dy_ref[...], over_rows, preferred_element_type=F32)


def expert_grads(me, place, parts, x, dy, shape, earlier, deps):
    experts, width, ff = shape
    fb = parts[0].shape[1]
    rows = x.shape[0]
    wide = pl.BlockSpec((1, width, fb), lambda k, m: (place, 0, m[0] ^ k))
    tall = pl.BlockSpec((1, fb, width), lambda k, m: (place, m[0] ^ k, 0))
    held = [*parts, x, dy]
    operands = [me, *held]
    specs = [whole(a) for a in held]
    aliases = {}
    if earlier is not None:
        aliases = {len(operands) + j: j for j in range(3)}
        operands += list(earlier)
        specs += [ANY] * 3
    need = 2 * sum(a.size for a in held) + 36 * width * fb
    need += 6 * rows * fb + 4 * rows * width
    return pl.pallas_call(
        grads_body,
        out_shape=(
            jax.ShapeDtypeStruct((experts, width, ff), F32),
            jax.ShapeDtypeStruct((experts, width, ff), F32),
            jax.ShapeDtypeStruct((experts, ff, width), F32),
            jax.ShapeDtypeStruct((8, 128), F32),
        ),
        grid_spec=pltpu.PrefetchScalarGridSpec(
            num_scalar_prefetch=1,
            grid=(ff // fb,),
            in_specs=specs + [ANY] * len(deps),
            out_specs=[wide, wide, tall, pl.BlockSpec((8, 128), lambda k, m: (0, 0))],
            scratch_shapes=[pltpu.VMEM((3, rows, fb), BF16)],
        ),
        input_output_aliases=aliases,
        compiler_params=params(need),
        cost_estimate=pl.CostEstimate(
            flops=6 * rows * width * ff, bytes_accessed=12 * width * ff, transcendentals=0
        ),
        name="expert_grads",
    )(*operands, *deps)


def swap(array, flip, count):
    return lax.ppermute(array, "expert", [(i, i ^ flip) for i in range(count)])


def plus(a, b):
    return (a.astype(F32) + b.astype(F32)).astype(BF16)


def event_order(chunks):
    events = []
    last = chunks - 1

    def begin(c):
        return PAIR * (c // 2) + WITHIN * (c % 2)

    for c in range(chunks):
        for step in range(6):
            events.append((begin(c) + step, c, step))
        terms = begin(c) + 6.1
        if c < last:
            terms = max(terms, begin(last) + 3.05 + c * 3.0 / chunks)
        events.append((terms, c, 6))
        events.append((terms + (0.01 if c < last else 9.0), c, 7))
    return [(c, step) for _, c, step in sorted(events)]


def shards(tokens, cotangent, gate_probs, expert_ids, gate_weight, up_weight, down_weight):
    count = lax.axis_size("expert")
    me = lax.axis_index("dp").astype(jnp.int32)
    group = lax.axis_index("expert").astype(jnp.int32)
    me_arg = me.reshape(1)
    local = gate_weight.shape[0]
    group_size, width = tokens.shape
    fb = gate_weight.shape[2] // lax.axis_size("dp")
    rows = count * CAP

    meta_rows = -(-group_size * TOP // width)
    pad_rows = -(-2 * meta_rows // 16) * 16

    def as_rows(a):
        flat = jnp.pad(a.astype(BF16).reshape(-1), (0, meta_rows * width - a.size))
        return flat.reshape(meta_rows, width)

    meta = jnp.concatenate(
        [
            as_rows(expert_ids),
            as_rows(gate_probs),
            jnp.zeros((pad_rows - 2 * meta_rows, width), BF16),
        ]
    )
    own_x = jnp.concatenate([tokens, meta])
    relative = list(range(0, count, 2)) + list(range(1, count, 2))
    chips = relative[: count // 2]

    def gathered(own):
        here = jnp.stack([own] + [swap(own, flip, count) for flip in chips[1:]])
        return jnp.concatenate([here, swap(here, 1, count)])

    all_x, all_dy = gathered(own_x), gathered(cotangent)

    def meta_of(which):
        part = all_x[:, group_size + which * meta_rows : group_size + (which + 1) * meta_rows]
        part = part.reshape(count, -1)[:, : group_size * TOP]
        return part.reshape(count, group_size, TOP).astype(F32)

    experts_here = (group * local + jnp.arange(local, dtype=jnp.int32)).astype(F32)
    before = (
        jnp.arange(group_size)[:, None] < jnp.arange(group_size)[None, :]
    ).astype(BF16)
    named = meta_of(0)[None] == experts_here[:, None, None, None]
    member = jnp.any(named, axis=3)
    prob = jnp.sum(jnp.where(named, meta_of(1)[None], 0.0), axis=3).reshape(local, -1)
    ranks = jnp.einsum(
        "egt,tu->egu", member.astype(BF16), before, preferred_element_type=F32
    ).astype(jnp.int32)
    first = CAP * jnp.arange(count, dtype=jnp.int32)[None, :, None]
    slots = jnp.where(member, ranks + first, -1).reshape(local, -1)
    flat_x = all_x[:, :group_size].reshape(-1, width)
    flat_dy = all_dy.reshape(-1, width)

    def chosen(e):
        return slots[e][None, :] == jnp.arange(rows, dtype=jnp.int32)[:, None]

    def gather(e):
        hot = chosen(e).astype(BF16)
        x = jnp.dot(hot, flat_x, preferred_element_type=F32).astype(BF16)
        dy32 = jnp.dot(hot, flat_dy, preferred_element_type=F32)
        g = jnp.sum(jnp.where(chosen(e), prob[e][None, :], 0.0), axis=1, keepdims=True)
        return x, dy32.astype(BF16), (dy32 * g).astype(BF16), g

    chunks = [gather(e) for e in range(local)]

    inward = [(0, 1), (3, 2)]
    outward = [(1, 0), (2, 3)]
    outer = [(0, 1), (1, 0), (2, 3), (3, 2)]
    inner = [(1, 2), (2, 1)]

    def move(a, pairs):
        return lax.ppermute(a, "dp", pairs)

    state = [dict() for _ in range(local)]
    chain = []
    grads = None
    row_terms = []
    for c, step in event_order(local):
        s = state[c]
        x, dy, scaled, g = chunks[c]
        if step == 0:
            s["p"] = forward(me_arg, x, dy, gate_weight, up_weight, down_weight, c, 1, chain)
            s["e3"] = move(s["p"][3], inward)
            chain = [s["p"][0]]
        elif step == 1:
            (out,) = add_blocks([s["p"][2], s["e3"]], chain)
            s["m2"] = move(out, inner)
            (second,) = pass_on([s["p"][2]], [out])
            s["e2"] = move(second, inward)
            chain = [out]
        elif step == 2:
            to_near, to_inner = add_blocks([s["p"][1], s["m2"], s["p"][3], s["e2"]], chain)
            s["near"], s["m3"] = move(to_near, outer), move(to_inner, inner)
            chain = [to_near]
        elif step == 3:
            own = hidden_units(s["p"][0], s["near"], s["m3"], g, chain)
            s["h0"], s["h1"], s["mid3"] = own, move(own, outer), move(own, inner)
            chain = [own]
        elif step == 4:
            s["h1"], s["mid3"] = pass_on([s["h1"], s["mid3"]], chain)
            s["mid2"], s["end2"] = move(s["h1"], inner), move(s["mid3"], outward)
            chain = [s["h1"]]
        elif step == 5:
            (s["mid2"],) = pass_on([s["mid2"]], chain)
            s["end3"] = move(s["mid2"], outward)
            chain = [s["mid2"]]
        else:
            parts = [s[k] for k in ("h0", "h1", "mid2", "end2", "mid3", "end3")]
            if step == 6:
                out = row_terms_of(me_arg, c, parts, rows, gate_weight, up_weight, chain)
                row_terms.append(out)
                chain = [out]
            else:
                *grads, token = expert_grads(
                    me_arg, c, parts, x, scaled, gate_weight.shape, grads, chain
                )
                chain = [token]

    middle = (me == 1) | (me == 2)

    def gate_sums(c):
        def part(name):
            a = state[c][name]
            return a[3 * rows :].reshape(-1, 16, fb)[:, 0].reshape(-1)[:rows].astype(F32)

        two = jnp.where(middle, part("mid2"), part("end2"))
        three = jnp.where(middle, part("mid3"), part("end3"))
        return part("h0") + part("h1") + two + three

    token_terms = 0.0
    gate_terms = []
    for e in range(local):
        token_terms = token_terms + lax.dot_general(
            chosen(e).astype(BF16), row_terms[e], (((0,), (0,)), ((), ())),
            preferred_element_type=F32,
        )
        gate_terms.append(jnp.sum(jnp.where(chosen(e), gate_sums(e)[:, None], 0.0), axis=0))

    gate_table = jnp.stack(gate_terms, axis=1).reshape(count, group_size, local)
    gate_table = gate_table.transpose(0, 2, 1).reshape(count, local * group_size)
    table_rows = -(-EXPERTS * group_size // width)
    table_pad = -(-table_rows // 16) * 16
    placed = lax.dynamic_update_slice(
        jnp.zeros((count, table_pad * width), BF16),
        gate_table.astype(BF16),
        (jnp.int32(0), group * local * group_size),
    ).reshape(count, table_pad, width)
    terms = token_terms.astype(BF16).reshape(count, group_size, width)
    terms = jnp.concatenate([terms, placed], axis=1)

    half_count = count // 2
    held = plus(terms[:half_count], swap(terms[half_count:], 1, count))

    def settle(part, order):
        have = chips
        for at, flip in enumerate(order):
            keep = [i for i, o in enumerate(have) if not o & flip]
            partner = [have.index(have[i] | flip) for i in keep]
            got = swap(jnp.stack([part[i] for i in partner]), flip, count)
            kept = jnp.stack([part[i] for i in keep])
            part = kept.astype(F32) + got.astype(F32)
            part = part if at == len(order) - 1 else part.astype(BF16)
            have = [have[i] for i in keep]
        return part[0]

    half = width // 2
    flips = [flip for flip in chips if flip and not flip & (flip - 1)]
    settled = jnp.concatenate(
        [settle(held[..., :half], flips), settle(held[..., half:], flips[::-1])], axis=1
    )
    grad_tokens = settled[:group_size].astype(BF16)
    table = settled[group_size:].reshape(-1)[: EXPERTS * group_size]
    table = table.reshape(EXPERTS, group_size).T
    hits = expert_ids[:, :, None] == jnp.arange(EXPERTS, dtype=jnp.int32)
    grad_gates = jnp.sum(jnp.where(hits, table[:, None, :], 0.0), axis=2)
    return (grad_tokens, grad_gates, *grads)


def solution(mesh):
    placed = (
        P("expert", "dp"),
        P("expert", "dp"),
        P("expert", None),
        P("expert", None),
        P("expert", "dp", None),
        P("expert", "dp", None),
        P("expert", None, "dp"),
    )
    return jax.shard_map(
        shards,
        mesh=mesh,
        in_specs=placed,
        out_specs=(
            P("expert", "dp"),
            P("expert", None),
            P("expert", "dp", None),
            P("expert", "dp", None),
            P("expert", None, "dp"),
        ),
        check_vma=False,
    )
```

```python
import functools

import jax
import jax.numpy as jnp
from jax import lax
from jax.experimental import pallas as pl
from jax.experimental.pallas import tpu as pltpu
from jax.sharding import PartitionSpec as P

TOP = 8
EXPERTS = 32
CAP = 36
MIB = 1024 * 1024
FORWARD_VMEM = 40 * MIB
BEGINS = (0.0, 0.5, 3.6, 5.2)
EARLY = 1.25
F32 = jnp.float32
BF16 = jnp.bfloat16
ANY = pl.BlockSpec(memory_space=pl.ANY)
VMEM = pl.BlockSpec(memory_space=pltpu.VMEM)


def params(need):
    return pltpu.CompilerParams(vmem_limit_bytes=min(60 * MIB, need + need // 4 + 4 * MIB))


def nt_dot(a, b):
    return lax.dot_general(a, b, (((1,), (1,)), ((), ())), preferred_element_type=F32)


def forward_body(me_ref, x_ref, dy_ref, gate_ref, up_ref, down_ref, *rest):
    outs = rest[-4:]
    fb = outs[0].shape[2]
    x, dy = x_ref[...], dy_ref[...]
    for at in range(4):
        block = pl.ds(pl.multiple_of((me_ref[0] ^ at) * fb, fb), fb)
        gate = jnp.dot(x, gate_ref[0, :, block], preferred_element_type=F32)
        up = jnp.dot(x, up_ref[0, :, block], preferred_element_type=F32)
        outs[at][0] = gate.astype(BF16)
        outs[at][1] = up.astype(BF16)
        outs[at][2] = nt_dot(dy, down_ref[0, block, :]).astype(BF16)


def forward(me, x, dy, gate_w, up_w, down_w, start, amount, deps):
    total, width = x.shape
    rows = total // amount
    blocks = 4
    ff = gate_w.shape[2]
    fb = ff // blocks
    held = pl.BlockSpec((rows, width), lambda i, m: (i, 0))
    wide = pl.BlockSpec((1, width, ff), lambda i, m: (start + i, 0, 0))
    tall = pl.BlockSpec((1, ff, width), lambda i, m: (start + i, 0, 0))
    part = jax.ShapeDtypeStruct((3, total, fb), BF16)
    return pl.pallas_call(
        forward_body,
        out_shape=[part] * blocks,
        grid_spec=pltpu.PrefetchScalarGridSpec(
            num_scalar_prefetch=1,
            grid=(amount,),
            in_specs=[held, held, wide, wide, tall] + [ANY] * len(deps),
            out_specs=[pl.BlockSpec((3, rows, fb), lambda i, m: (0, i, 0))] * blocks,
        ),
        compiler_params=params(FORWARD_VMEM),
        cost_estimate=pl.CostEstimate(
            flops=6 * total * width * ff,
            bytes_accessed=amount * 6 * width * ff,
            transcendentals=0,
        ),
        name="forward_products",
    )(me, x, dy, gate_w, up_w, down_w, *deps)


def add_body(pairs, *refs):
    outs = refs[-pairs:]
    for at in range(pairs):
        own, got = refs[2 * at], refs[2 * at + 1]
        outs[at][...] = (own[...].astype(F32) + got[...].astype(F32)).astype(BF16)


def add_blocks(terms, deps):
    pairs = len(terms) // 2
    size = terms[0].size
    return pl.pallas_call(
        functools.partial(add_body, pairs),
        out_shape=[jax.ShapeDtypeStruct(terms[0].shape, BF16)] * pairs,
        in_specs=[VMEM] * len(terms) + [ANY] * len(deps),
        out_specs=[VMEM] * pairs,
        compiler_params=params(pairs * 6 * size),
        cost_estimate=pl.CostEstimate(
            flops=pairs * size, bytes_accessed=pairs * 6 * size, transcendentals=0
        ),
        name="hop_sum",
    )(*terms, *deps)


def hidden_body(own_ref, near_ref, far_ref, g_ref, *rest):
    out_ref = rest[-1]
    rows, fb = own_ref.shape[1:]

    def total(at):
        return own_ref[at].astype(F32) + near_ref[at].astype(F32) + far_ref[at].astype(F32)

    gate, up, back = total(0), total(1), total(2)
    sig = jax.nn.sigmoid(gate)
    swish = gate * sig
    hidden = (swish * up).astype(BF16)
    product = back * hidden.astype(F32)
    grad = g_ref[...] * back
    out_ref[0:rows] = hidden
    out_ref[rows : 2 * rows] = (grad * up * (sig * (1.0 + gate * (1.0 - sig)))).astype(BF16)
    out_ref[2 * rows : 3 * rows] = (grad * swish).astype(BF16)
    high = product.astype(BF16)
    low = (product - high.astype(F32)).astype(BF16)
    ones = jnp.ones((16, fb), BF16)
    for part in range(-(-rows // fb)):
        lo, hi = part * fb, min(rows, part * fb + fb)
        sums = nt_dot(ones, high[lo:hi]) + nt_dot(ones, low[lo:hi])
        base = 3 * rows + 16 * part
        if hi - lo < fb:
            out_ref[base : base + 16] = jnp.zeros((16, fb), BF16)
        out_ref[base : base + 16, 0 : hi - lo] = sums.astype(BF16)


def hidden_units(own, near, far, g_rows, deps):
    _, rows, fb = own.shape
    tall = 3 * rows + 16 * (-(-rows // fb))
    return pl.pallas_call(
        hidden_body,
        out_shape=jax.ShapeDtypeStruct((tall, fb), BF16),
        in_specs=[VMEM] * 4 + [ANY] * len(deps),
        out_specs=VMEM,
        compiler_params=params(24 * rows * fb + 48 * rows * fb),
        cost_estimate=pl.CostEstimate(
            flops=30 * rows * fb, bytes_accessed=24 * rows * fb, transcendentals=rows * fb
        ),
        name="hidden_units",
    )(own, near, far, g_rows, *deps)


def pass_body(*refs):
    pass


def pass_on(arrays, deps):
    count = len(arrays)
    return pl.pallas_call(
        pass_body,
        out_shape=[jax.ShapeDtypeStruct(a.shape, a.dtype) for a in arrays],
        in_specs=[ANY] * (count + len(deps)),
        out_specs=[ANY] * count,
        input_output_aliases={at: at for at in range(count)},
        compiler_params=params(0),
        cost_estimate=pl.CostEstimate(flops=0, bytes_accessed=0, transcendentals=0),
        name="hop_forward",
    )(*arrays, *deps)


def take_blocks(step, me, parts, act, kinds, extra=None):
    middle = (me == 1) | (me == 2)
    rows = act.shape[1]

    def fill_when(wanted, source):
        @pl.when(wanted)
        def _():
            for at, j in enumerate(kinds):
                act[at] = source[pl.ds(j * rows, rows)]
            if extra is not None:
                extra[...] = source[pl.ds(3 * rows, extra.shape[0])]

    fill_when(step == 0, parts[0])
    fill_when(step == 1, parts[1])
    fill_when((step == 2) & middle, parts[2])
    fill_when((step == 2) & jnp.logical_not(middle), parts[3])
    fill_when((step == 3) & middle, parts[4])
    fill_when((step == 3) & jnp.logical_not(middle), parts[5])


def rows_body(me_ref, *refs):
    gate_ref, up_ref = refs[6:8]
    rows_ref, sums_ref, act, extra, total = refs[-5:]
    step = pl.program_id(0)
    take_blocks(step, me_ref[0], refs[:6], act, (1, 2), extra)
    terms = nt_dot(act[0], gate_ref[0]) + nt_dot(act[1], up_ref[0])

    @pl.when(step == 0)
    def _():
        total[...] = terms
        sums_ref[...] = extra[...].astype(F32)

    @pl.when(step > 0)
    def _():
        sums_ref[...] += extra[...].astype(F32)

    @pl.when((step > 0) & (step < 3))
    def _():
        total[...] += terms

    @pl.when(step == 3)
    def _():
        rows_ref[...] = (total[...] + terms).astype(BF16)


def whole(a):
    return pl.BlockSpec(a.shape, lambda k, m: (0,) * a.ndim, pipeline_mode=pl.Buffered(1))


def row_terms_of(me, place, parts, rows, gate_w, up_w, deps):
    _, width, ff = gate_w.shape
    fb = parts[0].shape[1]
    wide = pl.BlockSpec((1, width, fb), lambda k, m: (place, 0, m[0] ^ k))
    need = 2 * sum(a.size for a in parts) + 8 * width * fb + 4 * rows * width
    need += 4 * rows * fb + 16 * rows * width
    spare = parts[0].shape[0] - 3 * rows
    return pl.pallas_call(
        rows_body,
        out_shape=(
            jax.ShapeDtypeStruct((rows, width), BF16),
            jax.ShapeDtypeStruct((spare, fb), F32),
        ),
        grid_spec=pltpu.PrefetchScalarGridSpec(
            num_scalar_prefetch=1,
            grid=(ff // fb,),
            in_specs=[whole(a) for a in parts] + [wide, wide] + [ANY] * len(deps),
            out_specs=[
                pl.BlockSpec((rows, width), lambda k, m: (0, 0)),
                pl.BlockSpec((spare, fb), lambda k, m: (0, 0)),
            ],
            scratch_shapes=[
                pltpu.VMEM((2, rows, fb), BF16),
                pltpu.VMEM((spare, fb), BF16),
                pltpu.VMEM((rows, width), F32),
            ],
        ),
        compiler_params=params(need),
        cost_estimate=pl.CostEstimate(
            flops=4 * rows * width * ff, bytes_accessed=4 * width * ff, transcendentals=0
        ),
        name="input_terms",
    )(me, *parts, gate_w, up_w, *deps)


def grads_body(me_ref, *refs):
    x_ref, dy_ref = refs[6:8]
    grad_gate, grad_up, grad_down, token, act = refs[-5:]
    step = pl.program_id(0)

    @pl.when(step == 0)
    def _():
        token[...] = jnp.zeros_like(token)

    take_blocks(step, me_ref[0], refs[:6], act, (0, 1, 2))
    over_rows = (((0,), (0,)), ((), ()))
    grad_gate[0] = lax.dot_general(x_ref[...], act[1], over_rows, preferred_element_type=F32)
    grad_up[0] = lax.dot_general(x_ref[...], act[2], over_rows, preferred_element_type=F32)
    grad_down[0] = lax.dot_general(act[0], dy_ref[...], over_rows, preferred_element_type=F32)


def expert_grads(me, place, parts, x, dy, shape, earlier, deps):
    experts, width, ff = shape
    fb = parts[0].shape[1]
    rows = x.shape[0]
    wide = pl.BlockSpec((1, width, fb), lambda k, m: (place, 0, m[0] ^ k))
    tall = pl.BlockSpec((1, fb, width), lambda k, m: (place, m[0] ^ k, 0))
    held = [*parts, x, dy]
    operands = [me, *held]
    specs = [whole(a) for a in held]
    aliases = {}
    if earlier is not None:
        aliases = {len(operands) + j: j for j in range(3)}
        operands += list(earlier)
        specs += [ANY] * 3
    need = 2 * sum(a.size for a in held) + 36 * width * fb
    need += 6 * rows * fb + 4 * rows * width
    return pl.pallas_call(
        grads_body,
        out_shape=(
            jax.ShapeDtypeStruct((experts, width, ff), F32),
            jax.ShapeDtypeStruct((experts, width, ff), F32),
            jax.ShapeDtypeStruct((experts, ff, width), F32),
            jax.ShapeDtypeStruct((8, 128), F32),
        ),
        grid_spec=pltpu.PrefetchScalarGridSpec(
            num_scalar_prefetch=1,
            grid=(ff // fb,),
            in_specs=specs + [ANY] * len(deps),
            out_specs=[wide, wide, tall, pl.BlockSpec((8, 128), lambda k, m: (0, 0))],
            scratch_shapes=[pltpu.VMEM((3, rows, fb), BF16)],
        ),
        input_output_aliases=aliases,
        compiler_params=params(need),
        cost_estimate=pl.CostEstimate(
            flops=6 * rows * width * ff, bytes_accessed=12 * width * ff, transcendentals=0
        ),
        name="expert_grads",
    )(*operands, *deps)


def swap(array, flip, count):
    return lax.ppermute(array, "expert", [(i, i ^ flip) for i in range(count)])


def plus(a, b):
    return (a.astype(F32) + b.astype(F32)).astype(BF16)


def event_order(chunks):
    events = []
    last = chunks - 1

    def begin(c):
        return BEGINS[c] if c < len(BEGINS) else BEGINS[-1] + 2.0 * (c + 1 - len(BEGINS))

    for c in range(chunks):
        events.append((begin(c) - 0.01 if c < 2 else EARLY + 1.0 * (c - 2), c, -1))
        for step in range(6):
            events.append((begin(c) + step, c, step))
        terms = begin(c) + (7.1 if c < min(2, last) else 6.1)
        events.append((terms, c, 6))
        events.append((terms + (0.01 if c < last else 9.0), c, 7))
    return [(c, step) for _, c, step in sorted(events)]


def shards(tokens, cotangent, gate_probs, expert_ids, gate_weight, up_weight, down_weight):
    count = lax.axis_size("expert")
    me = lax.axis_index("dp").astype(jnp.int32)
    group = lax.axis_index("expert").astype(jnp.int32)
    me_arg = me.reshape(1)
    local = gate_weight.shape[0]
    group_size, width = tokens.shape
    fb = gate_weight.shape[2] // lax.axis_size("dp")
    rows = count * CAP

    meta_rows = -(-group_size * TOP // width)
    pad_rows = -(-2 * meta_rows // 16) * 16

    def as_rows(a):
        flat = jnp.pad(a.astype(BF16).reshape(-1), (0, meta_rows * width - a.size))
        return flat.reshape(meta_rows, width)

    meta = jnp.concatenate(
        [
            as_rows(expert_ids),
            as_rows(gate_probs),
            jnp.zeros((pad_rows - 2 * meta_rows, width), BF16),
        ]
    )
    own_x = jnp.concatenate([tokens, meta])
    relative = list(range(0, count, 2)) + list(range(1, count, 2))
    chips = relative[: count // 2]

    def gathered(own):
        here = jnp.stack([own] + [swap(own, flip, count) for flip in chips[1:]])
        return jnp.concatenate([here, swap(here, 1, count)])

    all_x, all_dy = gathered(own_x), gathered(cotangent)

    def meta_of(which):
        part = all_x[:, group_size + which * meta_rows : group_size + (which + 1) * meta_rows]
        part = part.reshape(count, -1)[:, : group_size * TOP]
        return part.reshape(count, group_size, TOP).astype(F32)

    experts_here = (group * local + jnp.arange(local, dtype=jnp.int32)).astype(F32)
    before = (
        jnp.arange(group_size)[:, None] < jnp.arange(group_size)[None, :]
    ).astype(BF16)
    named = meta_of(0)[None] == experts_here[:, None, None, None]
    member = jnp.any(named, axis=3)
    prob = jnp.sum(jnp.where(named, meta_of(1)[None], 0.0), axis=3).reshape(local, -1)
    ranks = jnp.einsum(
        "egt,tu->egu", member.astype(BF16), before, preferred_element_type=F32
    ).astype(jnp.int32)
    first = CAP * jnp.arange(count, dtype=jnp.int32)[None, :, None]
    slots = jnp.where(member, ranks + first, -1).reshape(local, -1)
    flat_x = all_x[:, :group_size].reshape(-1, width)
    flat_dy = all_dy.reshape(-1, width)

    def chosen(e):
        return slots[e][None, :] == jnp.arange(rows, dtype=jnp.int32)[:, None]

    def gather(e):
        hot = chosen(e).astype(BF16)
        x = jnp.dot(hot, flat_x, preferred_element_type=F32).astype(BF16)
        dy32 = jnp.dot(hot, flat_dy, preferred_element_type=F32)
        g = jnp.sum(jnp.where(chosen(e), prob[e][None, :], 0.0), axis=1, keepdims=True)
        return x, dy32.astype(BF16), (dy32 * g).astype(BF16), g

    chunks = [gather(e) for e in range(local)]

    inward = [(0, 1), (3, 2)]
    outward = [(1, 0), (2, 3)]
    outer = [(0, 1), (1, 0), (2, 3), (3, 2)]
    inner = [(1, 2), (2, 1)]

    def move(a, pairs):
        return lax.ppermute(a, "dp", pairs)

    state = [dict() for _ in range(local)]
    chain = []
    grads = None
    row_terms, gate_sums = [], []
    for c, step in event_order(local):
        s = state[c]
        x, dy, scaled, g = chunks[c]
        if step == -1:
            s["p"] = forward(me_arg, x, dy, gate_weight, up_weight, down_weight, c, 1, chain)
            chain = [s["p"][0]]
        elif step == 0:
            (first,) = pass_on([s["p"][3]], chain) if c > 1 else (s["p"][3],)
            s["e3"] = move(first, inward)
            s["p3"] = first
        elif step == 1:
            (out,) = add_blocks([s["p"][2], s["e3"]], chain)
            s["m2"] = move(out, inner)
            (second,) = pass_on([s["p"][2]], [out])
            s["e2"] = move(second, inward)
            chain = [out]
        elif step == 2:
            to_near, to_inner = add_blocks([s["p"][1], s["m2"], s["p3"], s["e2"]], chain)
            s["near"], s["m3"] = move(to_near, outer), move(to_inner, inner)
            chain = [to_near]
        elif step == 3:
            own = hidden_units(s["p"][0], s["near"], s["m3"], g, chain)
            s["h0"], s["h1"], s["mid3"] = own, move(own, outer), move(own, inner)
            chain = [own]
        elif step == 4:
            s["h1"], s["mid3"] = pass_on([s["h1"], s["mid3"]], chain)
            s["mid2"], s["end2"] = move(s["h1"], inner), move(s["mid3"], outward)
            chain = [s["h1"]]
        elif step == 5:
            (s["mid2"],) = pass_on([s["mid2"]], chain)
            s["end3"] = move(s["mid2"], outward)
            chain = [s["mid2"]]
        else:
            parts = [s[k] for k in ("h0", "h1", "mid2", "end2", "mid3", "end3")]
            if step == 6:
                out, sums = row_terms_of(
                    me_arg, c, parts, rows, gate_weight, up_weight, chain
                )
                row_terms.append(out)
                gate_sums.append(sums.reshape(-1, 16, fb)[:, 0].reshape(-1)[:rows])
                chain = [out]
            else:
                *grads, token = expert_grads(
                    me_arg, c, parts, x, scaled, gate_weight.shape, grads, chain
                )
                chain = [token]

    token_terms = 0.0
    gate_terms = []
    for e in range(local):
        token_terms = token_terms + lax.dot_general(
            chosen(e).astype(BF16), row_terms[e], (((0,), (0,)), ((), ())),
            preferred_element_type=F32,
        )
        gate_terms.append(jnp.sum(jnp.where(chosen(e), gate_sums[e][:, None], 0.0), axis=0))

    gate_table = jnp.stack(gate_terms, axis=1).reshape(count, group_size, local)
    gate_table = gate_table.transpose(0, 2, 1).reshape(count, local * group_size)
    table_rows = -(-EXPERTS * group_size // width)
    table_pad = -(-table_rows // 16) * 16
    placed = lax.dynamic_update_slice(
        jnp.zeros((count, table_pad * width), BF16),
        gate_table.astype(BF16),
        (jnp.int32(0), group * local * group_size),
    ).reshape(count, table_pad, width)
    terms = token_terms.astype(BF16).reshape(count, group_size, width)
    terms = jnp.concatenate([terms, placed], axis=1)

    half_count = count // 2
    held = plus(terms[:half_count], swap(terms[half_count:], 1, count))

    def settle(part, order):
        have = chips
        for at, flip in enumerate(order):
            keep = [i for i, o in enumerate(have) if not o & flip]
            partner = [have.index(have[i] | flip) for i in keep]
            got = swap(jnp.stack([part[i] for i in partner]), flip, count)
            kept = jnp.stack([part[i] for i in keep])
            part = kept.astype(F32) + got.astype(F32)
            part = part if at == len(order) - 1 else part.astype(BF16)
            have = [have[i] for i in keep]
        return part[0]

    half = width // 2
    flips = [flip for flip in chips if flip and not flip & (flip - 1)]
    settled = jnp.concatenate(
        [settle(held[..., :half], flips), settle(held[..., half:], flips[::-1])], axis=1
    )
    grad_tokens = settled[:group_size].astype(BF16)
    table = settled[group_size:].reshape(-1)[: EXPERTS * group_size]
    table = table.reshape(EXPERTS, group_size).T
    hits = expert_ids[:, :, None] == jnp.arange(EXPERTS, dtype=jnp.int32)
    grad_gates = jnp.sum(jnp.where(hits, table[:, None, :], 0.0), axis=2)
    return (grad_tokens, grad_gates, *grads)


def solution(mesh):
    placed = (
        P("expert", "dp"),
        P("expert", "dp"),
        P("expert", None),
        P("expert", None),
        P("expert", "dp", None),
        P("expert", "dp", None),
        P("expert", None, "dp"),
    )
    return jax.shard_map(
        shards,
        mesh=mesh,
        in_specs=placed,
        out_specs=(
            P("expert", "dp"),
            P("expert", None),
            P("expert", "dp", None),
            P("expert", "dp", None),
            P("expert", None, "dp"),
        ),
        check_vma=False,
    )
```

```python
import functools

import jax
import jax.numpy as jnp
from jax import lax
from jax.experimental import pallas as pl
from jax.experimental.pallas import tpu as pltpu
from jax.sharding import PartitionSpec as P

TOP = 8
EXPERTS = 32
CAP = 36
MIB = 1024 * 1024
FORWARD_VMEM = 40 * MIB
BEGINS = (0.0, 0.5, 3.6, 5.2)
EARLY = 1.25
F32 = jnp.float32
BF16 = jnp.bfloat16
ANY = pl.BlockSpec(memory_space=pl.ANY)
VMEM = pl.BlockSpec(memory_space=pltpu.VMEM)


def params(need):
    return pltpu.CompilerParams(vmem_limit_bytes=min(60 * MIB, need + need // 4 + 4 * MIB))


def nt_dot(a, b):
    return lax.dot_general(a, b, (((1,), (1,)), ((), ())), preferred_element_type=F32)


def forward_body(me_ref, x_ref, dy_ref, gate_ref, up_ref, down_ref, *rest):
    outs = rest[-4:]
    fb = outs[0].shape[2]
    x, dy = x_ref[...], dy_ref[...]
    for at in range(4):
        block = pl.ds(pl.multiple_of((me_ref[0] ^ at) * fb, fb), fb)
        gate = jnp.dot(x, gate_ref[0, :, block], preferred_element_type=F32)
        up = jnp.dot(x, up_ref[0, :, block], preferred_element_type=F32)
        outs[at][0] = gate.astype(BF16)
        outs[at][1] = up.astype(BF16)
        outs[at][2] = nt_dot(dy, down_ref[0, block, :]).astype(BF16)


def forward(me, x, dy, gate_w, up_w, down_w, start, amount, deps):
    total, width = x.shape
    rows = total // amount
    blocks = 4
    ff = gate_w.shape[2]
    fb = ff // blocks
    held = pl.BlockSpec((rows, width), lambda i, m: (i, 0))
    wide = pl.BlockSpec((1, width, ff), lambda i, m: (start + i, 0, 0))
    tall = pl.BlockSpec((1, ff, width), lambda i, m: (start + i, 0, 0))
    part = jax.ShapeDtypeStruct((3, total, fb), BF16)
    return pl.pallas_call(
        forward_body,
        out_shape=[part] * blocks,
        grid_spec=pltpu.PrefetchScalarGridSpec(
            num_scalar_prefetch=1,
            grid=(amount,),
            in_specs=[held, held, wide, wide, tall] + [ANY] * len(deps),
            out_specs=[pl.BlockSpec((3, rows, fb), lambda i, m: (0, i, 0))] * blocks,
        ),
        compiler_params=params(FORWARD_VMEM),
        cost_estimate=pl.CostEstimate(
            flops=6 * total * width * ff,
            bytes_accessed=amount * 6 * width * ff,
            transcendentals=0,
        ),
        name="forward_products",
    )(me, x, dy, gate_w, up_w, down_w, *deps)


def add_body(pairs, *refs):
    outs = refs[-pairs:]
    for at in range(pairs):
        own, got = refs[2 * at], refs[2 * at + 1]
        outs[at][...] = (own[...].astype(F32) + got[...].astype(F32)).astype(BF16)


def add_blocks(terms, deps):
    pairs = len(terms) // 2
    size = terms[0].size
    return pl.pallas_call(
        functools.partial(add_body, pairs),
        out_shape=[jax.ShapeDtypeStruct(terms[0].shape, BF16)] * pairs,
        in_specs=[VMEM] * len(terms) + [ANY] * len(deps),
        out_specs=[VMEM] * pairs,
        compiler_params=params(pairs * 6 * size),
        cost_estimate=pl.CostEstimate(
            flops=pairs * size, bytes_accessed=pairs * 6 * size, transcendentals=0
        ),
        name="hop_sum",
    )(*terms, *deps)


def hidden_body(own_ref, near_ref, far_ref, g_ref, *rest):
    out_ref = rest[-1]
    rows, fb = own_ref.shape[1:]

    def total(at):
        return own_ref[at].astype(F32) + near_ref[at].astype(F32) + far_ref[at].astype(F32)

    gate, up, back = total(0), total(1), total(2)
    sig = jax.nn.sigmoid(gate)
    swish = gate * sig
    hidden = (swish * up).astype(BF16)
    product = back * hidden.astype(F32)
    grad = g_ref[...] * back
    out_ref[0:rows] = hidden
    out_ref[rows : 2 * rows] = (grad * up * (sig * (1.0 + gate * (1.0 - sig)))).astype(BF16)
    out_ref[2 * rows : 3 * rows] = (grad * swish).astype(BF16)
    high = product.astype(BF16)
    low = (product - high.astype(F32)).astype(BF16)
    ones = jnp.ones((16, fb), BF16)
    for part in range(-(-rows // fb)):
        lo, hi = part * fb, min(rows, part * fb + fb)
        sums = nt_dot(ones, high[lo:hi]) + nt_dot(ones, low[lo:hi])
        base = 3 * rows + 16 * part
        if hi - lo < fb:
            out_ref[base : base + 16] = jnp.zeros((16, fb), BF16)
        out_ref[base : base + 16, 0 : hi - lo] = sums.astype(BF16)


def hidden_units(own, near, far, g_rows, deps):
    _, rows, fb = own.shape
    tall = 3 * rows + 16 * (-(-rows // fb))
    return pl.pallas_call(
        hidden_body,
        out_shape=jax.ShapeDtypeStruct((tall, fb), BF16),
        in_specs=[VMEM] * 4 + [ANY] * len(deps),
        out_specs=VMEM,
        compiler_params=params(24 * rows * fb + 48 * rows * fb),
        cost_estimate=pl.CostEstimate(
            flops=30 * rows * fb, bytes_accessed=24 * rows * fb, transcendentals=rows * fb
        ),
        name="hidden_units",
    )(own, near, far, g_rows, *deps)


def pass_body(*refs):
    pass


def pass_on(arrays, deps):
    count = len(arrays)
    return pl.pallas_call(
        pass_body,
        out_shape=[jax.ShapeDtypeStruct(a.shape, a.dtype) for a in arrays],
        in_specs=[ANY] * (count + len(deps)),
        out_specs=[ANY] * count,
        input_output_aliases={at: at for at in range(count)},
        compiler_params=params(0),
        cost_estimate=pl.CostEstimate(flops=0, bytes_accessed=0, transcendentals=0),
        name="hop_forward",
    )(*arrays, *deps)


def take_blocks(step, me, parts, act, kinds, extra=None):
    middle = (me == 1) | (me == 2)
    rows = act.shape[1]

    def fill_when(wanted, source):
        @pl.when(wanted)
        def _():
            for at, j in enumerate(kinds):
                act[at] = source[pl.ds(j * rows, rows)]
            if extra is not None:
                extra[...] = source[pl.ds(3 * rows, extra.shape[0])]

    fill_when(step == 0, parts[0])
    fill_when(step == 1, parts[1])
    fill_when((step == 2) & middle, parts[2])
    fill_when((step == 2) & jnp.logical_not(middle), parts[3])
    fill_when((step == 3) & middle, parts[4])
    fill_when((step == 3) & jnp.logical_not(middle), parts[5])


def rows_body(me_ref, *refs):
    gate_ref, up_ref = refs[6:8]
    rows_ref, sums_ref, act, extra, total = refs[-5:]
    step = pl.program_id(0)
    take_blocks(step, me_ref[0], refs[:6], act, (1, 2), extra)
    terms = nt_dot(act[0], gate_ref[0]) + nt_dot(act[1], up_ref[0])

    @pl.when(step == 0)
    def _():
        total[...] = terms
        sums_ref[...] = extra[...].astype(F32)

    @pl.when(step > 0)
    def _():
        sums_ref[...] += extra[...].astype(F32)

    @pl.when((step > 0) & (step < 3))
    def _():
        total[...] += terms

    @pl.when(step == 3)
    def _():
        rows_ref[...] = (total[...] + terms).astype(BF16)


def whole(a):
    return pl.BlockSpec(a.shape, lambda k, m: (0,) * a.ndim, pipeline_mode=pl.Buffered(1))


def row_terms_of(me, place, parts, rows, gate_w, up_w, deps):
    _, width, ff = gate_w.shape
    fb = parts[0].shape[1]
    wide = pl.BlockSpec((1, width, fb), lambda k, m: (place, 0, m[0] ^ k))
    need = 2 * sum(a.size for a in parts) + 8 * width * fb + 4 * rows * width
    need += 4 * rows * fb + 16 * rows * width
    spare = parts[0].shape[0] - 3 * rows
    return pl.pallas_call(
        rows_body,
        out_shape=(
            jax.ShapeDtypeStruct((rows, width), BF16),
            jax.ShapeDtypeStruct((spare, fb), F32),
        ),
        grid_spec=pltpu.PrefetchScalarGridSpec(
            num_scalar_prefetch=1,
            grid=(ff // fb,),
            in_specs=[whole(a) for a in parts] + [wide, wide] + [ANY] * len(deps),
            out_specs=[
                pl.BlockSpec((rows, width), lambda k, m: (0, 0)),
                pl.BlockSpec((spare, fb), lambda k, m: (0, 0)),
            ],
            scratch_shapes=[
                pltpu.VMEM((2, rows, fb), BF16),
                pltpu.VMEM((spare, fb), BF16),
                pltpu.VMEM((rows, width), F32),
            ],
        ),
        compiler_params=params(need),
        cost_estimate=pl.CostEstimate(
            flops=4 * rows * width * ff, bytes_accessed=4 * width * ff, transcendentals=0
        ),
        name="input_terms",
    )(me, *parts, gate_w, up_w, *deps)


def grads_body(me_ref, *refs):
    x_ref, dy_ref = refs[6:8]
    grad_gate, grad_up, grad_down, token, act = refs[-5:]
    step = pl.program_id(0)

    @pl.when(step == 0)
    def _():
        token[...] = jnp.zeros_like(token)

    take_blocks(step, me_ref[0], refs[:6], act, (0, 1, 2))
    over_rows = (((0,), (0,)), ((), ()))
    grad_gate[0] = lax.dot_general(x_ref[...], act[1], over_rows, preferred_element_type=F32)
    grad_up[0] = lax.dot_general(x_ref[...], act[2], over_rows, preferred_element_type=F32)
    grad_down[0] = lax.dot_general(act[0], dy_ref[...], over_rows, preferred_element_type=F32)


def expert_grads(me, place, parts, x, dy, shape, earlier, deps):
    experts, width, ff = shape
    fb = parts[0].shape[1]
    rows = x.shape[0]
    wide = pl.BlockSpec((1, width, fb), lambda k, m: (place, 0, m[0] ^ k))
    tall = pl.BlockSpec((1, fb, width), lambda k, m: (place, m[0] ^ k, 0))
    held = [*parts, x, dy]
    operands = [me, *held]
    specs = [whole(a) for a in held]
    aliases = {}
    if earlier is not None:
        aliases = {len(operands) + j: j for j in range(3)}
        operands += list(earlier)
        specs += [ANY] * 3
    need = 2 * sum(a.size for a in held) + 36 * width * fb
    need += 6 * rows * fb + 4 * rows * width
    return pl.pallas_call(
        grads_body,
        out_shape=(
            jax.ShapeDtypeStruct((experts, width, ff), F32),
            jax.ShapeDtypeStruct((experts, width, ff), F32),
            jax.ShapeDtypeStruct((experts, ff, width), F32),
            jax.ShapeDtypeStruct((8, 128), F32),
        ),
        grid_spec=pltpu.PrefetchScalarGridSpec(
            num_scalar_prefetch=1,
            grid=(ff // fb,),
            in_specs=specs + [ANY] * len(deps),
            out_specs=[wide, wide, tall, pl.BlockSpec((8, 128), lambda k, m: (0, 0))],
            scratch_shapes=[pltpu.VMEM((3, rows, fb), BF16)],
        ),
        input_output_aliases=aliases,
        compiler_params=params(need),
        cost_estimate=pl.CostEstimate(
            flops=6 * rows * width * ff, bytes_accessed=12 * width * ff, transcendentals=0
        ),
        name="expert_grads",
    )(*operands, *deps)


def swap(array, flip, count):
    return lax.ppermute(array, "expert", [(i, i ^ flip) for i in range(count)])


def plus(a, b):
    return (a.astype(F32) + b.astype(F32)).astype(BF16)


def event_order(chunks):
    events = []
    last = chunks - 1

    def begin(c):
        return BEGINS[c] if c < len(BEGINS) else BEGINS[-1] + 2.0 * (c + 1 - len(BEGINS))

    for c in range(chunks):
        events.append((begin(c) - 0.01 if c < 2 else EARLY + 1.0 * (c - 2), c, -1))
        for step in range(6):
            events.append((begin(c) + step, c, step))
        terms = begin(c) + (7.1 if c < min(2, last) else 6.1)
        if 1 < c < last:
            terms = max(terms, begin(last) + 5.05)
        events.append((terms, c, 6))
        events.append((terms + (0.01 if c < last else 9.0), c, 7))
    return [(c, step) for _, c, step in sorted(events)]


def shards(tokens, cotangent, gate_probs, expert_ids, gate_weight, up_weight, down_weight):
    count = lax.axis_size("expert")
    me = lax.axis_index("dp").astype(jnp.int32)
    group = lax.axis_index("expert").astype(jnp.int32)
    me_arg = me.reshape(1)
    local = gate_weight.shape[0]
    group_size, width = tokens.shape
    fb = gate_weight.shape[2] // lax.axis_size("dp")
    rows = count * CAP

    meta_rows = -(-group_size * TOP // width)
    pad_rows = -(-2 * meta_rows // 16) * 16

    def as_rows(a):
        flat = jnp.pad(a.astype(BF16).reshape(-1), (0, meta_rows * width - a.size))
        return flat.reshape(meta_rows, width)

    meta = jnp.concatenate(
        [
            as_rows(expert_ids),
            as_rows(gate_probs),
            jnp.zeros((pad_rows - 2 * meta_rows, width), BF16),
        ]
    )
    own_x = jnp.concatenate([tokens, meta])
    relative = list(range(0, count, 2)) + list(range(1, count, 2))
    chips = relative[: count // 2]

    def gathered(own):
        here = jnp.stack([own] + [swap(own, flip, count) for flip in chips[1:]])
        return jnp.concatenate([here, swap(here, 1, count)])

    all_x, all_dy = gathered(own_x), gathered(cotangent)

    def meta_of(which):
        part = all_x[:, group_size + which * meta_rows : group_size + (which + 1) * meta_rows]
        part = part.reshape(count, -1)[:, : group_size * TOP]
        return part.reshape(count, group_size, TOP).astype(F32)

    experts_here = (group * local + jnp.arange(local, dtype=jnp.int32)).astype(F32)
    before = (
        jnp.arange(group_size)[:, None] < jnp.arange(group_size)[None, :]
    ).astype(BF16)
    named = meta_of(0)[None] == experts_here[:, None, None, None]
    member = jnp.any(named, axis=3)
    prob = jnp.sum(jnp.where(named, meta_of(1)[None], 0.0), axis=3).reshape(local, -1)
    ranks = jnp.einsum(
        "egt,tu->egu", member.astype(BF16), before, preferred_element_type=F32
    ).astype(jnp.int32)
    first = CAP * jnp.arange(count, dtype=jnp.int32)[None, :, None]
    slots = jnp.where(member, ranks + first, -1).reshape(local, -1)
    flat_x = all_x[:, :group_size].reshape(-1, width)
    flat_dy = all_dy.reshape(-1, width)

    def chosen(e):
        return slots[e][None, :] == jnp.arange(rows, dtype=jnp.int32)[:, None]

    def gather(e):
        hot = chosen(e).astype(BF16)
        x = jnp.dot(hot, flat_x, preferred_element_type=F32).astype(BF16)
        dy32 = jnp.dot(hot, flat_dy, preferred_element_type=F32)
        g = jnp.sum(jnp.where(chosen(e), prob[e][None, :], 0.0), axis=1, keepdims=True)
        return x, dy32.astype(BF16), (dy32 * g).astype(BF16), g

    chunks = [gather(e) for e in range(local)]

    inward = [(0, 1), (3, 2)]
    outward = [(1, 0), (2, 3)]
    outer = [(0, 1), (1, 0), (2, 3), (3, 2)]
    inner = [(1, 2), (2, 1)]

    def move(a, pairs):
        return lax.ppermute(a, "dp", pairs)

    state = [dict() for _ in range(local)]
    chain = []
    grads = None
    row_terms, gate_sums = [], []
    for c, step in event_order(local):
        s = state[c]
        x, dy, scaled, g = chunks[c]
        if step == -1:
            s["p"] = forward(me_arg, x, dy, gate_weight, up_weight, down_weight, c, 1, chain)
            chain = [s["p"][0]]
        elif step == 0:
            (first,) = pass_on([s["p"][3]], chain) if c > 1 else (s["p"][3],)
            s["e3"] = move(first, inward)
            s["p3"] = first
        elif step == 1:
            (out,) = add_blocks([s["p"][2], s["e3"]], chain)
            s["m2"] = move(out, inner)
            (second,) = pass_on([s["p"][2]], [out])
            s["e2"] = move(second, inward)
            chain = [out]
        elif step == 2:
            to_near, to_inner = add_blocks([s["p"][1], s["m2"], s["p3"], s["e2"]], chain)
            s["near"], s["m3"] = move(to_near, outer), move(to_inner, inner)
            chain = [to_near]
        elif step == 3:
            own = hidden_units(s["p"][0], s["near"], s["m3"], g, chain)
            s["h0"], s["h1"], s["mid3"] = own, move(own, outer), move(own, inner)
            chain = [own]
        elif step == 4:
            s["h1"], s["mid3"] = pass_on([s["h1"], s["mid3"]], chain)
            s["mid2"], s["end2"] = move(s["h1"], inner), move(s["mid3"], outward)
            chain = [s["h1"]]
        elif step == 5:
            (s["mid2"],) = pass_on([s["mid2"]], chain)
            s["end3"] = move(s["mid2"], outward)
            chain = [s["mid2"]]
        else:
            parts = [s[k] for k in ("h0", "h1", "mid2", "end2", "mid3", "end3")]
            if step == 6:
                out, sums = row_terms_of(
                    me_arg, c, parts, rows, gate_weight, up_weight, chain
                )
                row_terms.append(out)
                gate_sums.append(sums.reshape(-1, 16, fb)[:, 0].reshape(-1)[:rows])
                chain = [out]
            else:
                *grads, token = expert_grads(
                    me_arg, c, parts, x, scaled, gate_weight.shape, grads, chain
                )
                chain = [token]

    token_terms = 0.0
    gate_terms = []
    for e in range(local):
        token_terms = token_terms + lax.dot_general(
            chosen(e).astype(BF16), row_terms[e], (((0,), (0,)), ((), ())),
            preferred_element_type=F32,
        )
        gate_terms.append(jnp.sum(jnp.where(chosen(e), gate_sums[e][:, None], 0.0), axis=0))

    gate_table = jnp.stack(gate_terms, axis=1).reshape(count, group_size, local)
    gate_table = gate_table.transpose(0, 2, 1).reshape(count, local * group_size)
    table_rows = -(-EXPERTS * group_size // width)
    table_pad = -(-table_rows // 16) * 16
    placed = lax.dynamic_update_slice(
        jnp.zeros((count, table_pad * width), BF16),
        gate_table.astype(BF16),
        (jnp.int32(0), group * local * group_size),
    ).reshape(count, table_pad, width)
    terms = token_terms.astype(BF16).reshape(count, group_size, width)
    terms = jnp.concatenate([terms, placed], axis=1)

    half_count = count // 2
    held = plus(terms[:half_count], swap(terms[half_count:], 1, count))

    def settle(part, order):
        have = chips
        for at, flip in enumerate(order):
            keep = [i for i, o in enumerate(have) if not o & flip]
            partner = [have.index(have[i] | flip) for i in keep]
            got = swap(jnp.stack([part[i] for i in partner]), flip, count)
            kept = jnp.stack([part[i] for i in keep])
            part = kept.astype(F32) + got.astype(F32)
            part = part if at == len(order) - 1 else part.astype(BF16)
            have = [have[i] for i in keep]
        return part[0]

    half = width // 2
    flips = [flip for flip in chips if flip and not flip & (flip - 1)]
    settled = jnp.concatenate(
        [settle(held[..., :half], flips), settle(held[..., half:], flips[::-1])], axis=1
    )
    grad_tokens = settled[:group_size].astype(BF16)
    table = settled[group_size:].reshape(-1)[: EXPERTS * group_size]
    table = table.reshape(EXPERTS, group_size).T
    hits = expert_ids[:, :, None] == jnp.arange(EXPERTS, dtype=jnp.int32)
    grad_gates = jnp.sum(jnp.where(hits, table[:, None, :], 0.0), axis=2)
    return (grad_tokens, grad_gates, *grads)


def solution(mesh):
    placed = (
        P("expert", "dp"),
        P("expert", "dp"),
        P("expert", None),
        P("expert", None),
        P("expert", "dp", None),
        P("expert", "dp", None),
        P("expert", None, "dp"),
    )
    return jax.shard_map(
        shards,
        mesh=mesh,
        in_specs=placed,
        out_specs=(
            P("expert", "dp"),
            P("expert", None),
            P("expert", "dp", None),
            P("expert", "dp", None),
            P("expert", None, "dp"),
        ),
        check_vma=False,
    )
```
